32 devices in a mesh: dp: 2 (over core), ctx: 8 (over z, y), fsdp: 2 (over x).
Axes of the slice: x: 2, y: 2, z: 4, core: 2. Of those that a mesh axis runs over, the one named last changes fastest.
Arguments:
- tokens: bfloat16 [4, 1536, 1024], P(('dp', 'fsdp'), 'ctx'), may hold values from -6 to 6
- attn_gain: bfloat16 [1024], P('fsdp'), may hold values from 0.099609375 to 1.8984375
- qkv_weight: bfloat16 [1024, 3072], P('fsdp'), may hold values from -0.21875 to 0.21875
- out_weight: bfloat16 [1024, 1024], P('fsdp'), may hold values from -3 to 3
- mlp_gain: bfloat16 [1024], P('fsdp'), may hold values from 0.099609375 to 1.8984375
- in_weight: bfloat16 [1024, 5248], P('fsdp'), may hold values from -0.1875 to 0.1875
- down_weight: bfloat16 [2624, 1024], P('fsdp'), may hold values from -0.125 to 0.125
- cotangent: bfloat16 [4, 1536, 1024], P(('dp', 'fsdp'), 'ctx'), may hold values from -6 to 6
Outputs:
- output: bfloat16 [4, 1536, 1024], P(('dp', 'fsdp'), 'ctx')
- grad_tokens: float32 [4, 1536, 1024], P(('dp', 'fsdp'), 'ctx')
- grad_attn_gain: float32 [1024], P('fsdp')
- grad_qkv_weight: float32 [1024, 3072], P('fsdp')
- grad_out_weight: float32 [1024, 1024], P('fsdp')
- grad_mlp_gain: float32 [1024], P('fsdp')
- grad_in_weight: float32 [1024, 5248], P('fsdp')
- grad_down_weight: float32 [2624, 1024], P('fsdp')
The draws below stay inside these ranges and needn't reach their ends.
All inputs are finite; a program needn't handle non-finite values.
Results may differ from the reference program's by a relative error of at most 0.02.
Values may be sent and summed in bfloat16 or wider, within the bound.
A program may use at most 192 MiB of HBM per device.

```python
import jax
import jax.numpy as jnp
from jax import lax

D = 1024
HEADS = 16
HEAD_DIM = 64
FF = 2624
LENGTH = 1536
SEQS = 4
N_CTX = 8


def level_of(stream_key, dims, pieces, smallest, largest):
    level = 1.0
    for dim, blocks in pieces:
        draws = jax.random.uniform(jax.random.fold_in(jax.random.fold_in(stream_key, 6), dim), (blocks,), jnp.float32, smallest / len(pieces), largest / len(pieces))
        level = level * jnp.repeat(jnp.exp(draws), dims[dim] // blocks).reshape((-1,) + (1,) * (len(dims) - 1 - dim))
    return level


def gaussian(rng, dims, deviation, reach, cuts=(), dtype=jnp.bfloat16):
    entries = jax.random.normal(rng, dims, jnp.float32) * deviation
    if len(cuts) > 0:
        entries = level_of(rng, dims, cuts, -0.22, 0.18) * entries
    return jnp.clip(entries, min=-reach, max=reach).astype(dtype)


def setup_inputs(seed: int = 0) -> dict:
    key_list = jax.random.split(jax.random.key(seed), 9)
    tokens = gaussian(key_list[0], (SEQS, LENGTH, D), 1.0, 6.0, ((0, 4), (1, 8)))
    attn_gain = jnp.clip(1.0 + 0.18 * jax.random.normal(key_list[1], (D,), jnp.float32), 0.099609375, 1.8984375).astype(jnp.bfloat16)
    qkv_weight = gaussian(key_list[2], (D, 3 * D), (2 * D // 3) ** -0.5, 0.21875, ((0, 2),))
    out_weight = gaussian(key_list[3], (D, D), (max(1, 7 * D // LENGTH)) ** -0.5, 3.0, ((0, 2),))
    mlp_gain = jnp.clip(1.0 + 0.18 * jax.random.normal(key_list[4], (D,), jnp.float32), 0.099609375, 1.8984375).astype(jnp.bfloat16)
    in_weight = gaussian(key_list[5], (D, 2 * FF), D ** -0.5, 0.1875, ((0, 2),))
    down_weight = gaussian(key_list[6], (FF, D), FF ** -0.5, 0.125, ((0, 2),))
    cotangent = gaussian(key_list[7], (SEQS, LENGTH, D), 1.0, 6.0, ((0, 4), (1, 8)))
    return {"tokens": tokens, "attn_gain": attn_gain, "qkv_weight": qkv_weight, "out_weight": out_weight, "mlp_gain": mlp_gain, "in_weight": in_weight, "down_weight": down_weight, "cotangent": cotangent}


theta_base = 160000.0
epsilon = 1e-05

@jax.custom_vjp
def low(v):
    return lax.optimization_barrier(v.astype(jnp.bfloat16)).astype(jnp.float32)

@jax.custom_vjp
def low_back(v):
    return v

def low_keep(v):
    return (low(v), None)

def low_pass(kept, grad):
    return (grad,)

def back_keep(v):
    return (v, None)

def back_low(kept, grad):
    return (low(grad),)
low.defvjp(low_keep, low_pass)
low_back.defvjp(back_keep, back_low)

def layer_norm(values, gain):
    centred = values - lax.optimization_barrier(jnp.mean(values, -1, keepdims=True))
    spread = lax.optimization_barrier(jnp.mean(centred * centred, -1, keepdims=True))
    return centred * lax.rsqrt(spread + epsilon) * gain

def rope_tables(positions, head_size):
    middle = head_size // 2
    inverse = theta_base ** (-(jnp.arange(middle).astype(jnp.float32) * 2.0) / head_size)
    angles = positions[:, None] * inverse[None, :]
    cosine = jnp.cos(angles)
    sine = jnp.sin(angles)
    return (jnp.concatenate([cosine, cosine], -1), jnp.concatenate([sine, sine], -1))

def rotate(values, cosine, sine):
    middle = values.shape[-1] // 2
    turned = jnp.concatenate([-values[..., middle:], values[..., :middle]], -1)
    return values * cosine[:, None, :] + turned * sine[:, None, :]

def geglu(expanded):
    middle = expanded.shape[-1] // 2
    return jax.nn.gelu(expanded[:, :middle], approximate=False) * expanded[:, middle:]

def precise_dot(left, right):
    return jnp.dot(left, right, precision=lax.Precision.HIGHEST)

def attend(queries, keys, values):
    length, heads, head_size = queries.shape
    scale = head_size ** (-0.5)
    blocked = queries.reshape(N_CTX, length // N_CTX, heads, head_size)

    def one_block(block):
        scores = low_back(jnp.einsum('qhe,khe->hqk', block, keys, precision=lax.Precision.HIGHEST) * scale)
        probs = low(jax.nn.softmax(scores, axis=-1))
        return jnp.einsum('hqk,khe->qhe', probs, values, precision=lax.Precision.HIGHEST)
    return lax.map(jax.checkpoint(one_block), blocked).reshape(length, heads * head_size)

def one_sequence(inputs, gain_one, w_qkv, w_out, gain_two, w_in, w_down, cosine, sine):
    length = inputs.shape[0]
    shaped = (length, HEADS, HEAD_DIM)
    normed = low(layer_norm(inputs, gain_one))
    projected = low_back(precise_dot(normed, w_qkv))
    queries = low(rotate(projected[:, :D].reshape(shaped), cosine, sine))
    keys = low(rotate(projected[:, D:2 * D].reshape(shaped), cosine, sine))
    values = low(projected[:, 2 * D:].reshape(shaped))
    attended = low(low_back(attend(queries, keys, values)))
    residual = inputs + low_back(precise_dot(attended, w_out))
    normed_mlp = low(layer_norm(residual, gain_two))
    expanded = low_back(precise_dot(normed_mlp, w_in))
    gated = low(geglu(expanded))
    return residual + low_back(precise_dot(gated, w_down))

def reference(tokens, attn_gain, qkv_weight, out_weight, mlp_gain, in_weight, down_weight, cotangent):
    positions = jnp.arange(LENGTH).astype(jnp.float32)
    cosine, sine = rope_tables(positions, HEAD_DIM)

    def forward(inputs, gain_one, w_qkv, w_out, gain_two, w_in, w_down):

        def per_sequence(row):
            return one_sequence(row, gain_one, w_qkv, w_out, gain_two, w_in, w_down, cosine, sine)
        return lax.map(per_sequence, inputs)
    output, pullback = jax.vjp(forward, tokens.astype(jnp.float32), attn_gain.astype(jnp.float32), qkv_weight.astype(jnp.float32), out_weight.astype(jnp.float32), mlp_gain.astype(jnp.float32), in_weight.astype(jnp.float32), down_weight.astype(jnp.float32))
    grads = pullback(cotangent.astype(jnp.float32))
    return (output.astype(jnp.bfloat16), grads[0], grads[1], grads[2], grads[3], grads[4], grads[5], grads[6])
```

```python
import jax
import jax.numpy as jnp
from jax import lax
from jax.sharding import PartitionSpec as P

HEAD_DIM = 64
LONGEST_UNROLLED = 8


theta_base = 160000.0
epsilon = 1e-05


def layer_norm(values, gain):
    centred = values - jnp.mean(values, -1, keepdims=True)
    spread = jnp.mean(centred * centred, -1, keepdims=True)
    return centred * lax.rsqrt(spread + epsilon) * gain


def rope_tables(positions, head_size):
    middle = head_size // 2
    inverse = theta_base ** (-(jnp.arange(middle).astype(jnp.float32) * 2.0) / head_size)
    angles = positions[:, None] * inverse[None, :]
    cosine = jnp.cos(angles)
    sine = jnp.sin(angles)
    return (jnp.concatenate([cosine, cosine], -1), jnp.concatenate([sine, sine], -1))


def rotate(values, cosine, sine):
    middle = values.shape[-1] // 2
    turned = jnp.concatenate([-values[..., middle:], values[..., :middle]], -1)
    return values * cosine[:, None, :] + turned * sine[:, None, :]


def unrotate(grads_in, cosine, sine):
    middle = grads_in.shape[-1] // 2
    scaled = grads_in * sine[:, None, :]
    return grads_in * cosine[:, None, :] + jnp.concatenate(
        [scaled[..., middle:], -scaled[..., :middle]], -1
    )


def geglu(expanded):
    middle = expanded.shape[-1] // 2
    return jax.nn.gelu(expanded[:, :middle], approximate=False) * expanded[:, middle:]


def ring_place(index, count):
    return index // 2 if index % 2 == 0 else count - 1 - index // 2


def ring_pairs(count, steps):
    at = sorted(range(count), key=lambda index: ring_place(index, count))
    return [(at[place], at[(place + steps) % count]) for place in range(count)]


def along_ring(value, steps):
    return lax.ppermute(value, "ctx", ring_pairs(lax.axis_size("ctx"), steps))


def swap(value, axis):
    return lax.ppermute(value, axis, [(0, 1), (1, 0)])


def fetch_rows(shard):
    part = shard.shape[0] // 2
    half = lax.dynamic_slice_in_dim(shard, lax.axis_index("dp") * part, part, 0)
    return lax.all_gather(swap(half, "fsdp"), "dp", axis=0, tiled=True)


def halves_of(values, first):
    middle = values.shape[1] // 2
    low, high = values[:, :middle], values[:, middle:]
    return jnp.where(first, low, high), jnp.where(first, high, low)


def join_halves(own, other, first):
    return jnp.where(first, jnp.concatenate([own, other], 1), jnp.concatenate([other, own], 1))


def dot_rows(values, own, other, first):
    mine, others = halves_of(values, first)
    return jnp.dot(mine, own, preferred_element_type=jnp.float32) + jnp.dot(
        others, other, preferred_element_type=jnp.float32
    )


def dot_rows_back(grads, own, other, first):
    mine = jnp.einsum("tg,fg->tf", grads, own, preferred_element_type=jnp.float32)
    others = jnp.einsum("tg,fg->tf", grads, other, preferred_element_type=jnp.float32)
    return join_halves(mine, others, first)


def add_low(left, right):
    return (left.astype(jnp.float32) + right.astype(jnp.float32)).astype(jnp.bfloat16)


def pick(values, number, axis):
    return lax.dynamic_index_in_dim(values, number, axis, keepdims=False)


def reduce_rows(grads):
    rows, columns = grads.shape
    core, shard = lax.axis_index("dp"), lax.axis_index("fsdp")
    quarters = grads.astype(jnp.bfloat16).reshape(2, 2, rows // 4, columns)
    summed = add_low(pick(quarters, core, 1), swap(pick(quarters, 1 - core, 1), "dp"))
    summed = add_low(pick(summed, shard, 0), swap(pick(summed, 1 - shard, 0), "fsdp"))
    if summed.shape[0] % (lax.axis_size("ctx") * 8):
        summed = summed.reshape(-1, 128)
    piece = lax.psum_scatter(summed, "ctx", scatter_dimension=0, tiled=True)
    shared = lax.all_gather(piece, ("dp", "ctx"), axis=0, tiled=True)
    return shared.reshape(rows // 2, columns).astype(jnp.float32)


def attend_block(queries, paired, state, scale):
    best, total, summed = state
    scores = (
        jnp.einsum("qhe,khe->hqk", queries, paired[0], preferred_element_type=jnp.float32) * scale
    )
    peak = jnp.maximum(best, jnp.max(scores, -1))
    shrink = jnp.exp(best - peak)
    weights = jnp.exp(scores - peak[..., None])
    total = total * shrink + jnp.sum(weights, -1)
    update = jnp.einsum(
        "hqk,khe->qhe", weights.astype(jnp.bfloat16), paired[1], preferred_element_type=jnp.float32
    )
    summed = summed * jnp.transpose(shrink)[:, :, None] + update
    return (peak, total, summed)


def back_block(queries, grad_attended, log_total, delta, paired, grad_queries, scale):
    scores = (
        jnp.einsum("qhe,khe->hqk", queries, paired[0], preferred_element_type=jnp.float32) * scale
    )
    probs = jnp.exp(scores - log_total[..., None])
    grad_probs = jnp.einsum(
        "qhe,khe->hqk", grad_attended, paired[1], preferred_element_type=jnp.float32
    )
    grad_scores = (probs * (grad_probs - delta[..., None])).astype(jnp.bfloat16)
    grad_values = jnp.einsum(
        "hqk,qhe->khe",
        probs.astype(jnp.bfloat16),
        grad_attended,
        preferred_element_type=jnp.float32,
    )
    grad_keys = (
        jnp.einsum("hqk,qhe->khe", grad_scores, queries, preferred_element_type=jnp.float32) * scale
    )
    grad_queries = (
        grad_queries
        + jnp.einsum("hqk,khe->qhe", grad_scores, paired[0], preferred_element_type=jnp.float32)
        * scale
    )
    return (jnp.stack([grad_keys, grad_values]), grad_queries)


def local(tokens, attn_gain, qkv_weight, out_weight, mlp_gain, in_weight, down_weight, cotangent):
    row_count = tokens.shape[1]
    cycle_size = lax.axis_size("ctx")
    first = lax.axis_index("fsdp") == 0
    gains = jnp.stack([attn_gain, mlp_gain]).astype(jnp.float32)
    gains = join_halves(gains, swap(gains, "fsdp"), first)
    gain_att, gain_mlp = gains[0], gains[1]
    other_qkv = fetch_rows(qkv_weight)
    other_out = fetch_rows(out_weight)
    other_in = fetch_rows(in_weight)
    other_down = fetch_rows(down_weight)
    width = out_weight.shape[1]
    head_size = HEAD_DIM
    heads = width // head_size
    shaped = (row_count, heads, head_size)
    scale = head_size ** (-0.5)
    inputs = tokens[0].astype(jnp.float32)
    positions = (lax.axis_index("ctx") * row_count + jnp.arange(row_count, dtype=jnp.int32)).astype(
        jnp.float32
    )
    cosine, sine = rope_tables(positions, head_size)
    normed = layer_norm(inputs, gain_att).astype(jnp.bfloat16)
    projected = dot_rows(normed, qkv_weight, other_qkv, first)
    queries = rotate(projected[:, :width].reshape(shaped), cosine, sine).astype(jnp.bfloat16)
    keys = rotate(projected[:, width : 2 * width].reshape(shaped), cosine, sine).astype(
        jnp.bfloat16
    )
    values = projected[:, 2 * width :].astype(jnp.bfloat16)
    local_pair = jnp.concatenate([keys.reshape(row_count, width), values], 1)

    def as_heads(blocks):
        joined = jnp.concatenate(blocks, 0)
        split = joined.reshape(joined.shape[0], 2, heads, head_size)
        return (split[:, 0], split[:, 1])

    state = (
        jnp.full((heads, row_count), -1e30, jnp.float32),
        jnp.zeros((heads, row_count), jnp.float32),
        jnp.zeros(shaped, jnp.float32),
    )
    unrolled = cycle_size <= LONGEST_UNROLLED
    groups = [[local_pair]]
    if unrolled:
        before, after = local_pair, local_pair
        for step in range(1, cycle_size // 2 + 1):
            before = along_ring(before, 1)
            group = [before]
            if step < cycle_size // 2:
                after = along_ring(after, -1)
                group.append(after)
            state = attend_block(queries, as_heads(groups[-1]), state, scale)
            groups.append(group)
        best, total, summed = attend_block(queries, as_heads(groups[-1]), state, scale)
    else:

        def forward_turn(number, carry):
            state, paired = carry
            return (
                attend_block(queries, as_heads([paired]), state, scale),
                along_ring(paired, 1),
            )

        state, paired = lax.fori_loop(0, cycle_size - 1, forward_turn, (state, local_pair))
        best, total, summed = attend_block(queries, as_heads([paired]), state, scale)
    attended = summed / jnp.transpose(total)[:, :, None]
    log_total = best + jnp.log(total)
    attended_low = attended.reshape(row_count, width).astype(jnp.bfloat16)
    residual = inputs + dot_rows(attended_low, out_weight, other_out, first)
    normed_mlp = layer_norm(residual, gain_mlp).astype(jnp.bfloat16)
    expanded = dot_rows(normed_mlp, in_weight, other_in, first)
    gated = geglu(expanded).astype(jnp.bfloat16)
    output = residual + dot_rows(gated, down_weight, other_down, first)
    grad_output = cotangent[0]
    grad_down = jnp.einsum("tf,td->fd", gated, grad_output, preferred_element_type=jnp.float32)
    grad_gated = dot_rows_back(grad_output, down_weight, other_down, first)
    unused_gate, pull_gate = jax.vjp(geglu, expanded)
    grad_expanded = pull_gate(grad_gated)[0].astype(jnp.bfloat16)
    grad_in = jnp.einsum("tf,tg->fg", normed_mlp, grad_expanded, preferred_element_type=jnp.float32)
    grad_normed_mlp = dot_rows_back(grad_expanded, in_weight, other_in, first)
    unused_mlp, pull_mlp = jax.vjp(layer_norm, residual, gain_mlp)
    grad_residual_mlp, grad_gain_mlp = pull_mlp(grad_normed_mlp)
    grad_residual = grad_output.astype(jnp.float32) + grad_residual_mlp
    grad_branch = grad_residual.astype(jnp.bfloat16)
    grad_wout = jnp.einsum(
        "tf,td->fd", attended_low, grad_branch, preferred_element_type=jnp.float32
    )
    grad_attended = (
        dot_rows_back(grad_branch, out_weight, other_out, first).astype(jnp.bfloat16).reshape(shaped)
    )
    delta = jnp.einsum("qhe,qhe->hq", grad_attended.astype(jnp.float32), attended)

    grad_queries = jnp.zeros(shaped, jnp.float32)

    def back_pair(blocks, grad_queries):
        grad_pair, grad_queries = back_block(
            queries, grad_attended, log_total, delta, as_heads(blocks), grad_queries, scale
        )
        return jnp.transpose(grad_pair, (1, 0, 2, 3)).reshape(-1, 2 * width), grad_queries

    if unrolled:
        forth, back = None, None
        for step in range(cycle_size // 2, -1, -1):
            grad_pair, grad_queries = back_pair(groups[step], grad_queries)
            if step == 0:
                grad_pair = grad_pair + forth.astype(jnp.float32) + back.astype(jnp.float32)
                break
            if step == cycle_size // 2:
                forth = along_ring(grad_pair.astype(jnp.bfloat16), 1)
                continue
            ahead = grad_pair[row_count:] + forth.astype(jnp.float32)
            behind = grad_pair[:row_count]
            if back is not None:
                behind = behind + back.astype(jnp.float32)
            forth = along_ring(ahead.astype(jnp.bfloat16), 1)
            back = along_ring(behind.astype(jnp.bfloat16), -1)
    else:

        def backward_turn(number, carry):
            paired_now, sent, grad_queries = carry
            grad_pair, grad_queries = back_pair([paired_now], grad_queries)
            grad_pair = (grad_pair + sent.astype(jnp.float32)).astype(jnp.bfloat16)
            return (along_ring(paired_now, 1), along_ring(grad_pair, 1), grad_queries)

        start_back = (local_pair, jnp.zeros_like(local_pair), grad_queries)
        unused_pair, sent, grad_queries = lax.fori_loop(
            0, cycle_size, backward_turn, start_back
        )
        grad_pair = sent.astype(jnp.float32)
    grad_projected = jnp.concatenate(
        [
            unrotate(grad_queries, cosine, sine).reshape(row_count, width),
            unrotate(grad_pair[:, :width].reshape(shaped), cosine, sine).reshape(row_count, width),
            grad_pair[:, width:],
        ],
        1,
    ).astype(jnp.bfloat16)
    grad_wqkv = jnp.einsum("tf,tg->fg", normed, grad_projected, preferred_element_type=jnp.float32)
    grad_normed = dot_rows_back(grad_projected, qkv_weight, other_qkv, first)
    unused_att, pull_att = jax.vjp(layer_norm, inputs, gain_att)
    grad_inputs_att, grad_gain_att = pull_att(grad_normed)
    grad_inputs = grad_residual + grad_inputs_att
    grad_gains = lax.psum(jnp.stack([grad_gain_att, grad_gain_mlp]), ("dp", "ctx", "fsdp"))
    grad_gains, unused_half = halves_of(grad_gains, first)
    return (
        output.astype(jnp.bfloat16)[None],
        grad_inputs[None],
        grad_gains[0],
        reduce_rows(grad_wqkv),
        reduce_rows(grad_wout),
        grad_gains[1],
        reduce_rows(grad_in),
        reduce_rows(grad_down),
    )


def solution(mesh):
    in_specs = (
        P(("dp", "fsdp"), "ctx", None),
        P("fsdp"),
        P("fsdp", None),
        P("fsdp", None),
        P("fsdp"),
        P("fsdp", None),
        P("fsdp", None),
        P(("dp", "fsdp"), "ctx", None),
    )
    out_specs = (
        P(("dp", "fsdp"), "ctx", None),
        P(("dp", "fsdp"), "ctx", None),
        P("fsdp"),
        P("fsdp", None),
        P("fsdp", None),
        P("fsdp"),
        P("fsdp", None),
        P("fsdp", None),
    )
    return jax.shard_map(local, mesh=mesh, in_specs=in_specs, out_specs=out_specs, check_vma=False)
```

```python
import jax
import jax.numpy as jnp
from jax import lax
from jax.sharding import PartitionSpec as P

HEAD_DIM = 64
LONGEST_UNROLLED = 8


theta_base = 160000.0
epsilon = 1e-05


def layer_norm(values, gain):
    centred = values - jnp.mean(values, -1, keepdims=True)
    spread = jnp.mean(centred * centred, -1, keepdims=True)
    return centred * lax.rsqrt(spread + epsilon) * gain


def rope_tables(positions, head_size):
    middle = head_size // 2
    inverse = theta_base ** (-(jnp.arange(middle).astype(jnp.float32) * 2.0) / head_size)
    angles = positions[:, None] * inverse[None, :]
    cosine = jnp.cos(angles)
    sine = jnp.sin(angles)
    return (jnp.concatenate([cosine, cosine], -1), jnp.concatenate([sine, sine], -1))


def rotate(values, cosine, sine):
    middle = values.shape[-1] // 2
    turned = jnp.concatenate([-values[..., middle:], values[..., :middle]], -1)
    return values * cosine[:, None, :] + turned * sine[:, None, :]


def unrotate(grads_in, cosine, sine):
    middle = grads_in.shape[-1] // 2
    scaled = grads_in * sine[:, None, :]
    return grads_in * cosine[:, None, :] + jnp.concatenate(
        [scaled[..., middle:], -scaled[..., :middle]], -1
    )


def geglu(expanded):
    middle = expanded.shape[-1] // 2
    return jax.nn.gelu(expanded[:, :middle], approximate=False) * expanded[:, middle:]


def ring_place(index, count):
    return index // 2 if index % 2 == 0 else count - 1 - index // 2


def ring_pairs(count, steps):
    at = sorted(range(count), key=lambda index: ring_place(index, count))
    return [(at[place], at[(place + steps) % count]) for place in range(count)]


def along_ring(value, steps):
    return lax.ppermute(value, "ctx", ring_pairs(lax.axis_size("ctx"), steps))


def swap(value, axis):
    return lax.ppermute(value, axis, [(0, 1), (1, 0)])


def fetch_half(shard):
    part = shard.shape[0] // 2
    half = lax.dynamic_slice_in_dim(shard, lax.axis_index("dp") * part, part, 0)
    return swap(half, "fsdp")


def trade_halves(half):
    return lax.all_gather(half, "dp", axis=0, tiled=True)


def halves_of(values, first):
    middle = values.shape[1] // 2
    low, high = values[:, :middle], values[:, middle:]
    return jnp.where(first, low, high), jnp.where(first, high, low)


def join_halves(own, other, first):
    return jnp.where(first, jnp.concatenate([own, other], 1), jnp.concatenate([other, own], 1))


def dot_rows(values, own, other, first):
    mine, others = halves_of(values, first)
    return jnp.dot(mine, own, preferred_element_type=jnp.float32) + jnp.dot(
        others, other, preferred_element_type=jnp.float32
    )


def dot_rows_back(grads, own, other, first):
    mine = jnp.einsum("tg,fg->tf", grads, own, preferred_element_type=jnp.float32)
    others = jnp.einsum("tg,fg->tf", grads, other, preferred_element_type=jnp.float32)
    return join_halves(mine, others, first)


def add_low(left, right):
    return (left.astype(jnp.float32) + right.astype(jnp.float32)).astype(jnp.bfloat16)


def pick(values, number, axis):
    return lax.dynamic_index_in_dim(values, number, axis, keepdims=False)


def sum_cores(grads):
    rows, columns = grads.shape
    core = lax.axis_index("dp")
    quarters = grads.astype(jnp.bfloat16).reshape(2, 2, rows // 4, columns)
    return add_low(pick(quarters, core, 1), swap(pick(quarters, 1 - core, 1), "dp"))


def sum_shards(summed):
    shard = lax.axis_index("fsdp")
    summed = add_low(pick(summed, shard, 0), swap(pick(summed, 1 - shard, 0), "fsdp"))
    if summed.shape[0] % (lax.axis_size("ctx") * 8):
        summed = summed.reshape(-1, 128)
    return summed


def sum_blocks(summed):
    count = lax.axis_size("ctx")
    if count > LONGEST_UNROLLED:
        return lax.psum_scatter(summed, "ctx", scatter_dimension=0, tiled=True)
    pieces = summed.reshape(count, summed.shape[0] // count, summed.shape[1])
    index = lax.axis_index("ctx")
    place = index // 2 + (index % 2) * (count - 1 - 2 * (index // 2))

    def piece(steps):
        there = (place + steps + count) % count
        turned = there // (count // 2)
        return pick(pieces, 2 * there + turned * (2 * count - 1 - 4 * there), 0)

    forth, back = along_ring(piece(count // 2), 1), None
    for step in range(count // 2 - 1, 0, -1):
        forth = along_ring(add_low(piece(step), forth), 1)
        behind = piece(-step)
        back = along_ring(behind if back is None else add_low(behind, back), -1)
    total = piece(0).astype(jnp.float32) + forth.astype(jnp.float32)
    return (total + back.astype(jnp.float32)).astype(jnp.bfloat16)


def share_rows(piece, columns):
    shared = lax.all_gather(piece, ("dp", "ctx"), axis=0, tiled=True)
    return shared.reshape(-1, columns).astype(jnp.float32)


def attend_block(queries, paired, state, scale):
    best, total, summed = state
    scores = (
        jnp.einsum("qhe,khe->hqk", queries, paired[0], preferred_element_type=jnp.float32) * scale
    )
    peak = jnp.maximum(best, jnp.max(scores, -1))
    shrink = jnp.exp(best - peak)
    weights = jnp.exp(scores - peak[..., None])
    total = total * shrink + jnp.sum(weights, -1)
    update = jnp.einsum(
        "hqk,khe->qhe", weights.astype(jnp.bfloat16), paired[1], preferred_element_type=jnp.float32
    )
    summed = summed * jnp.transpose(shrink)[:, :, None] + update
    return (peak, total, summed)


def back_block(queries, grad_attended, log_total, delta, paired, grad_queries, scale):
    scores = (
        jnp.einsum("qhe,khe->hqk", queries, paired[0], preferred_element_type=jnp.float32) * scale
    )
    probs = jnp.exp(scores - log_total[..., None])
    grad_probs = jnp.einsum(
        "qhe,khe->hqk", grad_attended, paired[1], preferred_element_type=jnp.float32
    )
    grad_scores = (probs * (grad_probs - delta[..., None])).astype(jnp.bfloat16)
    grad_values = jnp.einsum(
        "hqk,qhe->khe",
        probs.astype(jnp.bfloat16),
        grad_attended,
        preferred_element_type=jnp.float32,
    )
    grad_keys = (
        jnp.einsum("hqk,qhe->khe", grad_scores, queries, preferred_element_type=jnp.float32) * scale
    )
    grad_queries = (
        grad_queries
        + jnp.einsum("hqk,khe->qhe", grad_scores, paired[0], preferred_element_type=jnp.float32)
        * scale
    )
    return (jnp.stack([grad_keys, grad_values]), grad_queries)


def local(tokens, attn_gain, qkv_weight, out_weight, mlp_gain, in_weight, down_weight, cotangent):
    row_count = tokens.shape[1]
    cycle_size = lax.axis_size("ctx")
    first = lax.axis_index("fsdp") == 0
    gains = jnp.stack([attn_gain, mlp_gain]).astype(jnp.float32)
    gains = join_halves(gains, swap(gains, "fsdp"), first)
    gain_att, gain_mlp = gains[0], gains[1]
    other_qkv = trade_halves(fetch_half(qkv_weight))
    half_out, half_in, half_down = (
        fetch_half(out_weight),
        fetch_half(in_weight),
        fetch_half(down_weight),
    )
    width = out_weight.shape[1]
    head_size = HEAD_DIM
    heads = width // head_size
    shaped = (row_count, heads, head_size)
    scale = head_size ** (-0.5)
    inputs = tokens[0].astype(jnp.float32)
    positions = (lax.axis_index("ctx") * row_count + jnp.arange(row_count, dtype=jnp.int32)).astype(
        jnp.float32
    )
    cosine, sine = rope_tables(positions, head_size)
    normed = layer_norm(inputs, gain_att).astype(jnp.bfloat16)
    projected = dot_rows(normed, qkv_weight, other_qkv, first)
    queries = rotate(projected[:, :width].reshape(shaped), cosine, sine).astype(jnp.bfloat16)
    keys = rotate(projected[:, width : 2 * width].reshape(shaped), cosine, sine).astype(
        jnp.bfloat16
    )
    values = projected[:, 2 * width :].astype(jnp.bfloat16)
    local_pair = jnp.concatenate([keys.reshape(row_count, width), values], 1)

    def as_heads(blocks):
        joined = jnp.concatenate(blocks, 0)
        split = joined.reshape(joined.shape[0], 2, heads, head_size)
        return (split[:, 0], split[:, 1])

    state = (
        jnp.full((heads, row_count), -1e30, jnp.float32),
        jnp.zeros((heads, row_count), jnp.float32),
        jnp.zeros(shaped, jnp.float32),
    )
    unrolled = cycle_size <= LONGEST_UNROLLED
    groups = [[local_pair]]
    if unrolled:
        before, after = local_pair, local_pair
        for step in range(1, cycle_size // 2 + 1):
            before = along_ring(before, 1)
            group = [before]
            if step < cycle_size // 2:
                after = along_ring(after, -1)
                group.append(after)
            if step == 3:
                queries, state, half_out, half_in = lax.optimization_barrier(
                    (queries, state, half_out, half_in)
                )
            if step == 4:
                queries, state, half_down = lax.optimization_barrier((queries, state, half_down))
            state = attend_block(queries, as_heads(groups[-1]), state, scale)
            groups.append(group)
        best, total, summed = attend_block(queries, as_heads(groups[-1]), state, scale)
    else:

        def forward_turn(number, carry):
            state, paired = carry
            return (
                attend_block(queries, as_heads([paired]), state, scale),
                along_ring(paired, 1),
            )

        state, paired = lax.fori_loop(0, cycle_size - 1, forward_turn, (state, local_pair))
        best, total, summed = attend_block(queries, as_heads([paired]), state, scale)
    other_out, other_in, other_down = (
        trade_halves(half_out),
        trade_halves(half_in),
        trade_halves(half_down),
    )
    attended = summed / jnp.transpose(total)[:, :, None]
    log_total = best + jnp.log(total)
    attended_low = attended.reshape(row_count, width).astype(jnp.bfloat16)
    residual = inputs + dot_rows(attended_low, out_weight, other_out, first)
    normed_mlp = layer_norm(residual, gain_mlp).astype(jnp.bfloat16)
    expanded = dot_rows(normed_mlp, in_weight, other_in, first)
    gated = geglu(expanded).astype(jnp.bfloat16)
    output = residual + dot_rows(gated, down_weight, other_down, first)
    grad_output = cotangent[0]
    grad_down = jnp.einsum("tf,td->fd", gated, grad_output, preferred_element_type=jnp.float32)
    grad_gated = dot_rows_back(grad_output, down_weight, other_down, first)
    unused_gate, pull_gate = jax.vjp(geglu, expanded)
    grad_expanded = pull_gate(grad_gated)[0].astype(jnp.bfloat16)
    grad_in = jnp.einsum("tf,tg->fg", normed_mlp, grad_expanded, preferred_element_type=jnp.float32)
    grad_normed_mlp = dot_rows_back(grad_expanded, in_weight, other_in, first)
    unused_mlp, pull_mlp = jax.vjp(layer_norm, residual, gain_mlp)
    grad_residual_mlp, grad_gain_mlp = pull_mlp(grad_normed_mlp)
    grad_residual = grad_output.astype(jnp.float32) + grad_residual_mlp
    grad_branch = grad_residual.astype(jnp.bfloat16)
    grad_wout = jnp.einsum(
        "tf,td->fd", attended_low, grad_branch, preferred_element_type=jnp.float32
    )
    grad_attended = (
        dot_rows_back(grad_branch, out_weight, other_out, first).astype(jnp.bfloat16).reshape(shaped)
    )
    delta = jnp.einsum("qhe,qhe->hq", grad_attended.astype(jnp.float32), attended)

    sum_down, sum_in, sum_out = sum_cores(grad_down), sum_cores(grad_in), sum_cores(grad_wout)
    if not unrolled:
        sum_down, sum_in, sum_out = sum_shards(sum_down), sum_shards(sum_in), sum_shards(sum_out)
    grad_queries = jnp.zeros(shaped, jnp.float32)

    def back_pair(blocks, grad_queries):
        grad_pair, grad_queries = back_block(
            queries, grad_attended, log_total, delta, as_heads(blocks), grad_queries, scale
        )
        return jnp.transpose(grad_pair, (1, 0, 2, 3)).reshape(-1, 2 * width), grad_queries

    if unrolled:
        forth, back = None, None
        for step in range(cycle_size // 2, -1, -1):
            if step == cycle_size // 2 - 1:
                grad_attended, grad_queries, sum_down, sum_in, sum_out = lax.optimization_barrier(
                    (grad_attended, grad_queries, sum_down, sum_in, sum_out)
                )
                sum_down = sum_shards(sum_down)
                sum_in = sum_shards(sum_in)
                sum_out = sum_shards(sum_out)
            if step == 0:
                grad_attended, grad_queries, sum_down, sum_in, sum_out = lax.optimization_barrier(
                    (grad_attended, grad_queries, sum_down, sum_in, sum_out)
                )
            grad_pair, grad_queries = back_pair(groups[step], grad_queries)
            if step == 0:
                grad_pair = grad_pair + forth.astype(jnp.float32) + back.astype(jnp.float32)
                break
            if step == cycle_size // 2:
                forth = along_ring(grad_pair.astype(jnp.bfloat16), 1)
                continue
            ahead = grad_pair[row_count:] + forth.astype(jnp.float32)
            behind = grad_pair[:row_count]
            if back is not None:
                behind = behind + back.astype(jnp.float32)
            forth = along_ring(ahead.astype(jnp.bfloat16), 1)
            back = along_ring(behind.astype(jnp.bfloat16), -1)
    else:

        def backward_turn(number, carry):
            paired_now, sent, grad_queries = carry
            grad_pair, grad_queries = back_pair([paired_now], grad_queries)
            grad_pair = (grad_pair + sent.astype(jnp.float32)).astype(jnp.bfloat16)
            return (along_ring(paired_now, 1), along_ring(grad_pair, 1), grad_queries)

        start_back = (local_pair, jnp.zeros_like(local_pair), grad_queries)
        unused_pair, sent, grad_queries = lax.fori_loop(
            0, cycle_size, backward_turn, start_back
        )
        grad_pair = sent.astype(jnp.float32)
    grad_projected = jnp.concatenate(
        [
            unrotate(grad_queries, cosine, sine).reshape(row_count, width),
            unrotate(grad_pair[:, :width].reshape(shaped), cosine, sine).reshape(row_count, width),
            grad_pair[:, width:],
        ],
        1,
    ).astype(jnp.bfloat16)
    grad_wqkv = jnp.einsum("tf,tg->fg", normed, grad_projected, preferred_element_type=jnp.float32)
    grad_normed = dot_rows_back(grad_projected, qkv_weight, other_qkv, first)
    unused_att, pull_att = jax.vjp(layer_norm, inputs, gain_att)
    grad_inputs_att, grad_gain_att = pull_att(grad_normed)
    grad_inputs = grad_residual + grad_inputs_att
    extra = jnp.stack([grad_gain_att, grad_gain_mlp], 1)
    extra = jnp.pad(extra, ((0, 0), (0, 126)))
    joined = jnp.concatenate([grad_wqkv.astype(jnp.bfloat16), extra.astype(jnp.bfloat16)], 1)
    summed_qkv = share_rows(sum_blocks(sum_shards(sum_cores(joined))), joined.shape[1])
    return (
        output.astype(jnp.bfloat16)[None],
        grad_inputs[None],
        summed_qkv[:, 3 * width],
        summed_qkv[:, : 3 * width],
        share_rows(sum_blocks(sum_out), grad_wout.shape[1]),
        summed_qkv[:, 3 * width + 1],
        share_rows(sum_blocks(sum_in), grad_in.shape[1]),
        share_rows(sum_blocks(sum_down), grad_down.shape[1]),
    )


def solution(mesh):
    in_specs = (
        P(("dp", "fsdp"), "ctx", None),
        P("fsdp"),
        P("fsdp", None),
        P("fsdp", None),
        P("fsdp"),
        P("fsdp", None),
        P("fsdp", None),
        P(("dp", "fsdp"), "ctx", None),
    )
    out_specs = (
        P(("dp", "fsdp"), "ctx", None),
        P(("dp", "fsdp"), "ctx", None),
        P("fsdp"),
        P("fsdp", None),
        P("fsdp", None),
        P("fsdp"),
        P("fsdp", None),
        P("fsdp", None),
    )
    return jax.shard_map(local, mesh=mesh, in_specs=in_specs, out_specs=out_specs, check_vma=False)
```

```python
import jax
import jax.numpy as jnp
from jax import lax
from jax.sharding import PartitionSpec as P

HEAD_DIM = 64
LONGEST_UNROLLED = 8


theta_base = 160000.0
epsilon = 1e-05


def layer_norm(values, gain):
    centred = values - jnp.mean(values, -1, keepdims=True)
    spread = jnp.mean(centred * centred, -1, keepdims=True)
    return centred * lax.rsqrt(spread + epsilon) * gain


def rope_tables(positions, head_size):
    middle = head_size // 2
    inverse = theta_base ** (-(jnp.arange(middle).astype(jnp.float32) * 2.0) / head_size)
    angles = positions[:, None] * inverse[None, :]
    cosine = jnp.cos(angles)
    sine = jnp.sin(angles)
    return (jnp.concatenate([cosine, cosine], -1), jnp.concatenate([sine, sine], -1))


def rotate(values, cosine, sine):
    middle = values.shape[-1] // 2
    turned = jnp.concatenate([-values[..., middle:], values[..., :middle]], -1)
    return values * cosine[:, None, :] + turned * sine[:, None, :]


def unrotate(grads_in, cosine, sine):
    middle = grads_in.shape[-1] // 2
    scaled = grads_in * sine[:, None, :]
    return grads_in * cosine[:, None, :] + jnp.concatenate(
        [scaled[..., middle:], -scaled[..., :middle]], -1
    )


def geglu(expanded):
    middle = expanded.shape[-1] // 2
    return jax.nn.gelu(expanded[:, :middle], approximate=False) * expanded[:, middle:]


def ring_place(index, count):
    return index // 2 if index % 2 == 0 else count - 1 - index // 2


def ring_pairs(count, steps):
    at = sorted(range(count), key=lambda index: ring_place(index, count))
    return [(at[place], at[(place + steps) % count]) for place in range(count)]


def along_ring(value, steps):
    return lax.ppermute(value, "ctx", ring_pairs(lax.axis_size("ctx"), steps))


def swap(value, axis):
    return lax.ppermute(value, axis, [(0, 1), (1, 0)])


def fetch_half(shard):
    part = shard.shape[0] // 2
    half = lax.dynamic_slice_in_dim(shard, lax.axis_index("dp") * part, part, 0)
    return swap(half, "fsdp")


def trade_halves(half):
    return lax.all_gather(half, "dp", axis=0, tiled=True)


def halves_of(values, first):
    middle = values.shape[1] // 2
    low, high = values[:, :middle], values[:, middle:]
    return jnp.where(first, low, high), jnp.where(first, high, low)


def join_halves(own, other, first):
    return jnp.where(first, jnp.concatenate([own, other], 1), jnp.concatenate([other, own], 1))


def dot_rows(values, own, other, first):
    mine, others = halves_of(values, first)
    return jnp.dot(mine, own, preferred_element_type=jnp.float32) + jnp.dot(
        others, other, preferred_element_type=jnp.float32
    )


def dot_rows_back(grads, own, other, first):
    mine = jnp.einsum("tg,fg->tf", grads, own, preferred_element_type=jnp.float32)
    others = jnp.einsum("tg,fg->tf", grads, other, preferred_element_type=jnp.float32)
    return join_halves(mine, others, first)


def add_low(left, right):
    return (left.astype(jnp.float32) + right.astype(jnp.float32)).astype(jnp.bfloat16)


def pick(values, number, axis):
    return lax.dynamic_index_in_dim(values, number, axis, keepdims=False)


def sum_cores(grads):
    rows, columns = grads.shape
    core = lax.axis_index("dp")
    quarters = grads.astype(jnp.bfloat16).reshape(2, 2, rows // 4, columns)
    return add_low(pick(quarters, core, 1), swap(pick(quarters, 1 - core, 1), "dp"))


def sum_shards(summed):
    shard = lax.axis_index("fsdp")
    summed = add_low(pick(summed, shard, 0), swap(pick(summed, 1 - shard, 0), "fsdp"))
    if summed.shape[0] % (lax.axis_size("ctx") * 8):
        summed = summed.reshape(-1, 128)
    return summed


def sum_blocks(summed):
    count = lax.axis_size("ctx")
    if count > LONGEST_UNROLLED:
        return lax.psum_scatter(summed, "ctx", scatter_dimension=0, tiled=True)
    pieces = summed.reshape(count, summed.shape[0] // count, summed.shape[1])
    index = lax.axis_index("ctx")
    place = index // 2 + (index % 2) * (count - 1 - 2 * (index // 2))

    def piece(steps):
        there = (place + steps + count) % count
        turned = there // (count // 2)
        return pick(pieces, 2 * there + turned * (2 * count - 1 - 4 * there), 0)

    forth, back = along_ring(piece(count // 2), 1), None
    for step in range(count // 2 - 1, 0, -1):
        forth = along_ring(add_low(piece(step), forth), 1)
        behind = piece(-step)
        back = along_ring(behind if back is None else add_low(behind, back), -1)
    total = piece(0).astype(jnp.float32) + forth.astype(jnp.float32)
    return (total + back.astype(jnp.float32)).astype(jnp.bfloat16)


def share_rows(piece, columns):
    shared = lax.all_gather(piece, ("dp", "ctx"), axis=0, tiled=True)
    return shared.reshape(-1, columns).astype(jnp.float32)


def attend_block(queries, paired, state, scale):
    best, total, summed = state
    scores = (
        jnp.einsum("qhe,khe->hqk", queries, paired[0], preferred_element_type=jnp.float32) * scale
    )
    peak = jnp.maximum(best, jnp.max(scores, -1))
    shrink = jnp.exp(best - peak)
    weights = jnp.exp(scores - peak[..., None])
    total = total * shrink + jnp.sum(weights, -1)
    update = jnp.einsum(
        "hqk,khe->qhe", weights.astype(jnp.bfloat16), paired[1], preferred_element_type=jnp.float32
    )
    summed = summed * jnp.transpose(shrink)[:, :, None] + update
    return (peak, total, summed)


def back_block(queries, grad_attended, log_total, delta, paired, grad_queries, scale):
    scores = (
        jnp.einsum("qhe,khe->hqk", queries, paired[0], preferred_element_type=jnp.float32) * scale
    )
    probs = jnp.exp(scores - log_total[..., None])
    grad_probs = jnp.einsum(
        "qhe,khe->hqk", grad_attended, paired[1], preferred_element_type=jnp.float32
    )
    grad_scores = (probs * (grad_probs - delta[..., None])).astype(jnp.bfloat16)
    grad_values = jnp.einsum(
        "hqk,qhe->khe",
        probs.astype(jnp.bfloat16),
        grad_attended,
        preferred_element_type=jnp.float32,
    )
    grad_keys = (
        jnp.einsum("hqk,qhe->khe", grad_scores, queries, preferred_element_type=jnp.float32) * scale
    )
    grad_queries = (
        grad_queries
        + jnp.einsum("hqk,khe->qhe", grad_scores, paired[0], preferred_element_type=jnp.float32)
        * scale
    )
    return (jnp.stack([grad_keys, grad_values]), grad_queries)


def local(tokens, attn_gain, qkv_weight, out_weight, mlp_gain, in_weight, down_weight, cotangent):
    row_count = tokens.shape[1]
    cycle_size = lax.axis_size("ctx")
    first = lax.axis_index("fsdp") == 0
    gains = jnp.stack([attn_gain, mlp_gain]).astype(jnp.float32)
    gains = join_halves(gains, swap(gains, "fsdp"), first)
    gain_att, gain_mlp = gains[0], gains[1]
    other_qkv = trade_halves(fetch_half(qkv_weight))
    half_out, half_in, half_down = (
        fetch_half(out_weight),
        fetch_half(in_weight),
        fetch_half(down_weight),
    )
    width = out_weight.shape[1]
    head_size = HEAD_DIM
    heads = width // head_size
    shaped = (row_count, heads, head_size)
    scale = head_size ** (-0.5)
    inputs = tokens[0].astype(jnp.float32)
    positions = (lax.axis_index("ctx") * row_count + jnp.arange(row_count, dtype=jnp.int32)).astype(
        jnp.float32
    )
    cosine, sine = rope_tables(positions, head_size)
    normed = layer_norm(inputs, gain_att).astype(jnp.bfloat16)
    projected = dot_rows(normed, qkv_weight, other_qkv, first)
    queries = rotate(projected[:, :width].reshape(shaped), cosine, sine).astype(jnp.bfloat16)
    keys = rotate(projected[:, width : 2 * width].reshape(shaped), cosine, sine).astype(
        jnp.bfloat16
    )
    values = projected[:, 2 * width :].astype(jnp.bfloat16)
    local_pair = jnp.concatenate([keys.reshape(row_count, width), values], 1)

    def as_heads(blocks):
        joined = jnp.concatenate(blocks, 0)
        split = joined.reshape(joined.shape[0], 2, heads, head_size)
        return (split[:, 0], split[:, 1])

    state = (
        jnp.full((heads, row_count), -1e30, jnp.float32),
        jnp.zeros((heads, row_count), jnp.float32),
        jnp.zeros(shaped, jnp.float32),
    )
    unrolled = 4 <= cycle_size <= LONGEST_UNROLLED
    groups = [[local_pair]]
    if unrolled:
        before, after = local_pair, local_pair
        for step in range(1, cycle_size // 2 + 1):
            before = along_ring(before, 1)
            group = [before]
            if step < cycle_size // 2:
                after = along_ring(after, -1)
                group.append(after)
            if step == 3:
                queries, state, half_out, half_in = lax.optimization_barrier(
                    (queries, state, half_out, half_in)
                )
            if step == 4:
                queries, state, half_down = lax.optimization_barrier((queries, state, half_down))
            state = attend_block(queries, as_heads(groups[-1]), state, scale)
            groups.append(group)
        best, total, summed = attend_block(queries, as_heads(groups[-1]), state, scale)
    else:

        def forward_turn(number, carry):
            state, paired = carry
            return (
                attend_block(queries, as_heads([paired]), state, scale),
                along_ring(paired, 1),
            )

        state, paired = lax.fori_loop(0, cycle_size - 1, forward_turn, (state, local_pair))
        best, total, summed = attend_block(queries, as_heads([paired]), state, scale)
    other_out, other_in, other_down = (
        trade_halves(half_out),
        trade_halves(half_in),
        trade_halves(half_down),
    )
    attended = summed / jnp.transpose(total)[:, :, None]
    log_total = best + jnp.log(total)
    attended_low = attended.reshape(row_count, width).astype(jnp.bfloat16)
    residual = inputs + dot_rows(attended_low, out_weight, other_out, first)
    normed_mlp = layer_norm(residual, gain_mlp).astype(jnp.bfloat16)
    expanded = dot_rows(normed_mlp, in_weight, other_in, first)
    gated = geglu(expanded).astype(jnp.bfloat16)
    output = residual + dot_rows(gated, down_weight, other_down, first)
    grad_output = cotangent[0]
    grad_down = jnp.einsum("tf,td->fd", gated, grad_output, preferred_element_type=jnp.float32)
    grad_gated = dot_rows_back(grad_output, down_weight, other_down, first)
    unused_gate, pull_gate = jax.vjp(geglu, expanded)
    grad_expanded = pull_gate(grad_gated)[0].astype(jnp.bfloat16)
    grad_in = jnp.einsum("tf,tg->fg", normed_mlp, grad_expanded, preferred_element_type=jnp.float32)
    grad_normed_mlp = dot_rows_back(grad_expanded, in_weight, other_in, first)
    unused_mlp, pull_mlp = jax.vjp(layer_norm, residual, gain_mlp)
    grad_residual_mlp, grad_gain_mlp = pull_mlp(grad_normed_mlp)
    grad_residual = grad_output.astype(jnp.float32) + grad_residual_mlp
    grad_branch = grad_residual.astype(jnp.bfloat16)
    grad_wout = jnp.einsum(
        "tf,td->fd", attended_low, grad_branch, preferred_element_type=jnp.float32
    )
    grad_attended = (
        dot_rows_back(grad_branch, out_weight, other_out, first).astype(jnp.bfloat16).reshape(shaped)
    )
    delta = jnp.einsum("qhe,qhe->hq", grad_attended.astype(jnp.float32), attended)

    sum_down, sum_in, sum_out = sum_cores(grad_down), sum_cores(grad_in), sum_cores(grad_wout)
    if not unrolled:
        sum_down, sum_in, sum_out = sum_shards(sum_down), sum_shards(sum_in), sum_shards(sum_out)
    grad_queries = jnp.zeros(shaped, jnp.float32)

    def back_pair(blocks, grad_queries):
        grad_pair, grad_queries = back_block(
            queries, grad_attended, log_total, delta, as_heads(blocks), grad_queries, scale
        )
        return jnp.transpose(grad_pair, (1, 0, 2, 3)).reshape(-1, 2 * width), grad_queries

    if unrolled:
        forth, back = None, None
        for step in range(cycle_size // 2, -1, -1):
            if step == cycle_size // 2 - 1:
                grad_attended, grad_queries, sum_down, sum_in, sum_out = lax.optimization_barrier(
                    (grad_attended, grad_queries, sum_down, sum_in, sum_out)
                )
                sum_down = sum_shards(sum_down)
                sum_out = sum_shards(sum_out)
            if step == cycle_size // 2 - 2:
                grad_attended, grad_queries, sum_in = lax.optimization_barrier(
                    (grad_attended, grad_queries, sum_in)
                )
                sum_in = sum_shards(sum_in)
            if step == 0:
                grad_attended, grad_queries, sum_down, sum_out = lax.optimization_barrier(
                    (grad_attended, grad_queries, sum_down, sum_out)
                )
            grad_pair, grad_queries = back_pair(groups[step], grad_queries)
            if step == 0:
                grad_pair = grad_pair + forth.astype(jnp.float32) + back.astype(jnp.float32)
                break
            if step == cycle_size // 2:
                forth = along_ring(grad_pair.astype(jnp.bfloat16), 1)
                continue
            ahead = grad_pair[row_count:] + forth.astype(jnp.float32)
            behind = grad_pair[:row_count]
            if back is not None:
                behind = behind + back.astype(jnp.float32)
            forth = along_ring(ahead.astype(jnp.bfloat16), 1)
            back = along_ring(behind.astype(jnp.bfloat16), -1)
    else:

        def backward_turn(number, carry):
            paired_now, sent, grad_queries = carry
            grad_pair, grad_queries = back_pair([paired_now], grad_queries)
            grad_pair = (grad_pair + sent.astype(jnp.float32)).astype(jnp.bfloat16)
            return (along_ring(paired_now, 1), along_ring(grad_pair, 1), grad_queries)

        start_back = (local_pair, jnp.zeros_like(local_pair), grad_queries)
        unused_pair, sent, grad_queries = lax.fori_loop(
            0, cycle_size, backward_turn, start_back
        )
        grad_pair = sent.astype(jnp.float32)
    grad_projected = jnp.concatenate(
        [
            unrotate(grad_queries, cosine, sine).reshape(row_count, width),
            unrotate(grad_pair[:, :width].reshape(shaped), cosine, sine).reshape(row_count, width),
            grad_pair[:, width:],
        ],
        1,
    ).astype(jnp.bfloat16)
    grad_wqkv = jnp.einsum("tf,tg->fg", normed, grad_projected, preferred_element_type=jnp.float32)
    grad_normed = dot_rows_back(grad_projected, qkv_weight, other_qkv, first)
    unused_att, pull_att = jax.vjp(layer_norm, inputs, gain_att)
    grad_inputs_att, grad_gain_att = pull_att(grad_normed)
    grad_inputs = grad_residual + grad_inputs_att
    extra = jnp.stack([grad_gain_att, grad_gain_mlp], 1)
    extra = jnp.pad(extra, ((0, 0), (0, 126)))
    joined = jnp.concatenate([grad_wqkv.astype(jnp.bfloat16), extra.astype(jnp.bfloat16)], 1)
    sum_qkv, sum_in = lax.optimization_barrier((sum_cores(joined), sum_in))
    summed_qkv = share_rows(sum_blocks(sum_shards(sum_qkv)), joined.shape[1])
    return (
        output.astype(jnp.bfloat16)[None],
        grad_inputs[None],
        summed_qkv[:, 3 * width],
        summed_qkv[:, : 3 * width],
        share_rows(sum_blocks(sum_out), grad_wout.shape[1]),
        summed_qkv[:, 3 * width + 1],
        share_rows(sum_blocks(sum_in), grad_in.shape[1]),
        share_rows(sum_blocks(sum_down), grad_down.shape[1]),
    )


def solution(mesh):
    in_specs = (
        P(("dp", "fsdp"), "ctx", None),
        P("fsdp"),
        P("fsdp", None),
        P("fsdp", None),
        P("fsdp"),
        P("fsdp", None),
        P("fsdp", None),
        P(("dp", "fsdp"), "ctx", None),
    )
    out_specs = (
        P(("dp", "fsdp"), "ctx", None),
        P(("dp", "fsdp"), "ctx", None),
        P("fsdp"),
        P("fsdp", None),
        P("fsdp", None),
        P("fsdp"),
        P("fsdp", None),
        P("fsdp", None),
    )
    return jax.shard_map(local, mesh=mesh, in_specs=in_specs, out_specs=out_specs, check_vma=False)
```
